32 devices in a mesh: grp: 2 (over x), band: 16 (over z, y, core).
Axes of the slice: x: 2, y: 2, z: 4, core: 2. Of those that a mesh axis runs over, the one named last changes fastest.
Arguments:
- source_field: bfloat16 [1024, 128, 256], P(('grp', 'band')), parts along dimension 0, may hold values from -6 to 6
- interp_weight: bfloat16 [1536, 128, 128], P('band'), may hold values from -0.5 to 0.5
- dest_band: int32 [1536, 1], P('band'), may hold values from 0 to 15; in each aligned block of 96 rows (0 to 95, 96 to 191, ...) at most 9 rows name the same one
- target_block: int32 [1536], P('band'), may hold values from 0 to 44
- source_block: int32 [1536], P('band'), may hold values from 0 to 31
- entry_count: int32 [16], P('band'), may hold values from 1 to 96, 1152 in all
- mode_index: int32 [384], replicated, may hold values from 0 to 720, as said below
- filter_weight: bfloat16 [64, 2, 384, 256], P(None, None, 'band'), may hold values from -4 to 4
Outputs:
- processed: bfloat16 [184320, 256], P(('grp', 'band')), parts along dimension 0
The draws below stay inside these ranges and needn't reach their ends.
There are 2 independent parts, one for each index of `grp`. The reference program is written for one: setup_inputs(seed, part) draws one part's arguments, and reference() takes and returns one part's arrays. A program takes and returns all parts, laid end to end along the dimension named above; an argument that names none is the same for every part. Nothing has to cross between parts.
Inputs may be any that keep to these rules, and one draw needn't show every extreme that they name: `dest_band`: among the entries of one device no band is named more than 9 times, a bound that some block reaches. `entry_count`: the counts sum to 1152; entries of a device past its count are padding. `mode_index`: distinct wavenumbers; 0 and 720 are always among them.
All inputs are finite; a program needn't handle non-finite values.
Results may differ from the reference program's by a relative error of at most 0.0076.
Values may be sent and summed in bfloat16 or wider, within the bound.
A program may use at most 128 MiB of HBM per device.

```python
import math
import jax
import jax.numpy as jnp
import numpy as np
from jax import lax

C = 256
NLON = 1440
MODES = 384
PIX = 128
SRC_DEV = 32
ENT_DEV = 96
CAP = 9
TB_DEV = 45
NLAT = 64
SRC_BLOCKS = 512
ENTRIES = 1536
VALID_TOTAL = 1152
N_BAND = 16


def draw_mode_index(key, part):
    key = jax.random.fold_in(key, 7)
    half = NLON // 2
    inner = jax.random.permutation(key, half - 1)[:MODES - 2] + 1
    chosen = jnp.concatenate([jnp.array([0, half], jnp.int32), inner.astype(jnp.int32)])
    order = jax.random.permutation(jax.random.fold_in(key, 1), MODES)
    return chosen[order]


def with_ends(entries, key, least, largest):
    shape = entries.shape
    spot = [jax.random.randint(jax.random.fold_in(key, axis), (), 0, shape[axis]) for axis in range(len(shape))]
    entries = entries.at[tuple(spot)].set(least)
    longest = shape.index(max(shape))
    spot[longest] = (spot[longest] + 1) % shape[longest]
    return entries.at[tuple(spot)].set(largest)


def steps_of(stream_key, shape, pieces, least, high):
    level, own = 1.0, jax.random.fold_in(stream_key, 6)
    for dim, blocks in pieces:
        heights = jnp.exp(jax.random.uniform(jax.random.fold_in(own, dim), (blocks,), jnp.float32, least / len(pieces), high / len(pieces)))
        level = level * jnp.repeat(heights, shape[dim] // blocks).reshape([-1 if axis == dim else 1 for axis in range(len(shape))])
    return level


def split_up(amount, total, reach, lean):
    weights = [(1 << 20) // math.isqrt(rank ** lean) + 1 for rank in range(2, amount + 1)]
    rest, counts = total - reach - (amount - 1), [1] * (amount - 1)
    while rest > 0:
        free = [i for i in range(amount - 1) if counts[i] < reach]
        pool, budget = sum([weights[i] for i in free]), rest
        for i in free:
            more = min(reach - counts[i], max(1, budget * weights[i] // pool), rest)
            counts[i] = counts[i] + more
            rest = rest - more
    return np.array([reach] + counts)


def uneven(stream_key, count, total, reach, skew):
    if count == 2:
        one = jax.random.randint(stream_key, (), max(1, total - reach), min(reach, total - 1) + 1)
        return jnp.stack([one, total - one])
    sizes = jnp.asarray(split_up(count, total, reach, skew), jnp.int32)
    couples = (count - 1) // 2
    giver, receiver = sizes[1:1 + 2 * couples:2], sizes[2:2 + 2 * couples:2]
    slack = jnp.minimum(giver - 1, reach - receiver)
    passed = jax.random.randint(jax.random.fold_in(stream_key, 1), (couples,), 0, 1 << 20) % (slack + 1)
    sizes = sizes.at[1:1 + 2 * couples:2].set(giver - passed).at[2:2 + 2 * couples:2].set(receiver + passed)
    return sizes[jax.random.permutation(jax.random.fold_in(stream_key, 2), count)]


def assign_block(key, own, number, rows, count, top, bound, slope):
    sequence = jax.random.permutation(key, count)
    heavy_load, common = shares(count, rows * top, bound, slope, True), shares(count, rows * top, bound, slope, False)
    places = jnp.arange(count)

    def named(lengths, turn):
        used = int((lengths > 0).sum())
        fixed = max(1, used // 4)
        moved = fixed + (places - fixed + turn * (used - fixed)) % max(1, count - fixed)
        return jnp.zeros((count,), jnp.int32).at[sequence[jnp.where(places < fixed, places, moved)]].set(jnp.asarray(lengths, jnp.int32))

    lengths = jnp.where(number % 4 == 0, named(heavy_load, number // 4), named(common, number - number // 4 - 1))
    mixed = jax.random.permutation(jax.random.fold_in(own, 3), count)
    source_of, taker = mixed[0:count // 2 * 2:2], mixed[1:count // 2 * 2:2]
    slack = jnp.minimum(lengths[source_of] - 1, bound - lengths[taker]) // 2
    slack = jnp.where((source_of == sequence[0]) | (taker == sequence[0]) | (lengths[taker] == 0), 0, jnp.maximum(slack, 0))
    moved = jax.random.randint(jax.random.fold_in(own, 4), (count // 2,), 0, 1 << 20) % (slack + 1)
    lengths = lengths.at[source_of].add(-moved).at[taker].add(moved)
    labels = jnp.searchsorted(jnp.cumsum(lengths), jnp.arange(rows * top), side="right").astype(jnp.int32)
    table = labels.reshape(top, rows).T
    table = table[jax.random.permutation(jax.random.fold_in(own, 1), rows)]
    turn = jax.random.randint(jax.random.fold_in(own, 2), (rows, 1), 0, top)
    return jnp.take_along_axis(table, (jnp.arange(top)[None, :] + turn) % top, axis=1)


def shares(count, total, limit, skew, full):
    portions = [(1 << 20) // math.isqrt(standing ** skew) + 1 for standing in range(1, count + 1)]
    largest = limit if full else min(limit, max(-(-total // count), total * portions[0] // sum(portions)))
    least = 1 if total - largest >= count - 1 else 0
    holding, spare = [largest] + [least] * (count - 1), total - largest - least * (count - 1)
    while spare > 0:
        candidates = [i for i in range(1, count) if holding[i] < largest] or [i for i in range(1, count) if holding[i] < limit]
        whole, left = sum([portions[i] for i in candidates]), spare
        for i in candidates:
            addition = min(limit - holding[i], max(1, left * portions[i] // whole), spare)
            holding[i] = holding[i] + addition
            spare = spare - addition
    return np.array(holding)


def centred(key, shape, spread, bound, split=(), held_as=jnp.bfloat16):
    factor_of = steps_of(key, shape, split, -0.22, 0.18) if split else 1.0
    result = jax.random.normal(key, shape, jnp.float32) * spread * factor_of
    return jnp.minimum(jnp.maximum(result, -bound), bound).astype(held_as)


def setup_inputs(seed: int = 0, part: int = 0) -> dict:
    key_of = jax.random.split(jax.random.key(seed), 9)
    part_keys = jax.random.split(jax.random.fold_in(key_of[8], part), 9)
    source_field = centred(part_keys[0], (SRC_BLOCKS, PIX, C), 1.0, 6.0, ((0, 16),))
    interp_weight = centred(key_of[1], (ENTRIES, PIX, PIX), PIX ** -0.5, 0.5, ((0, 16),))
    dest_band_keys = jax.random.split(jax.random.fold_in(key_of[2], 1), ENTRIES // ENT_DEV)
    dest_band_turns = jax.random.permutation(jax.random.fold_in(key_of[2], 3), ENTRIES // ENT_DEV)
    dest_band = jax.vmap(lambda own, number: assign_block(jax.random.fold_in(key_of[2], 2), own, number, ENT_DEV, N_BAND, 1, CAP, 2))(dest_band_keys, dest_band_turns).reshape((ENTRIES, 1))
    target_block = with_ends(jax.random.randint(key_of[3], (ENTRIES,), 0, TB_DEV), jax.random.fold_in(key_of[3], 1), 0, TB_DEV - 1).astype(jnp.int32)
    source_block = with_ends(jax.random.randint(key_of[4], (ENTRIES,), 0, SRC_DEV), jax.random.fold_in(key_of[4], 1), 0, SRC_DEV - 1).astype(jnp.int32)
    entry_count = uneven(key_of[5], N_BAND, VALID_TOTAL, ENT_DEV, 2).astype(jnp.int32)
    mode_index = draw_mode_index(jax.random.fold_in(key_of[8], 71), part)
    filter_weight = centred(key_of[7], (NLAT, 2, MODES, C), 1.0, 4.0, ((2, 16),))
    return {"source_field": source_field, "interp_weight": interp_weight, "dest_band": dest_band, "target_block": target_block, "source_block": source_block, "entry_count": entry_count, "mode_index": mode_index, "filter_weight": filter_weight}


def lon_tables(mode_index):
    grid_n = jnp.arange(NLON, dtype=jnp.int32)
    phase = grid_n[:, None] * mode_index[None, :] % NLON
    angle = phase.astype(jnp.float32) * (2.0 * math.pi / NLON)
    forward = jnp.concatenate([jnp.cos(angle), -jnp.sin(angle)], axis=1).astype(jnp.bfloat16)
    factor = jnp.where((mode_index == 0) | (mode_index == NLON // 2), 1.0, 2.0).astype(jnp.float32)
    inverse = jnp.concatenate([factor[None, :] * jnp.cos(angle), -factor[None, :] * jnp.sin(angle)], axis=1)
    return (forward, inverse.T.astype(jnp.bfloat16))

def lat_table(nlat):
    index = jnp.arange(nlat, dtype=jnp.int32)
    phase = index[:, None] * index[None, :] % nlat
    angle = phase.astype(jnp.float32) * (2.0 * math.pi / nlat)
    cosine = jnp.cos(angle)
    sine = jnp.sin(angle)
    upper = jnp.stack([cosine, sine], axis=2)
    lower = jnp.stack([-sine, cosine], axis=2)
    table = jnp.stack([upper, lower], axis=1)
    return table.reshape(2 * nlat, 2 * nlat).astype(jnp.bfloat16)

def reference(source_field, interp_weight, dest_band, target_block, source_block, entry_count, mode_index, filter_weight):
    dest = dest_band[:, 0]

    def per_device(accum, device):
        start = device * ENT_DEV
        weights = lax.dynamic_slice_in_dim(interp_weight, start, ENT_DEV, 0).astype(jnp.float32)
        src_ids = lax.dynamic_slice_in_dim(source_block, start, ENT_DEV, 0) + device * SRC_DEV
        pixels = jnp.take(source_field, src_ids.astype(jnp.int32), axis=0).astype(jnp.float32)
        made = jnp.einsum('eij,ejc->eic', weights, pixels)
        valid = (jnp.arange(ENT_DEV, dtype=jnp.int32) < entry_count[device]).astype(jnp.float32)
        made = (made * valid[:, None, None]).astype(jnp.bfloat16)
        made = lax.optimization_barrier(made).astype(jnp.float32)
        goal = lax.dynamic_slice_in_dim(dest, start, ENT_DEV, 0) * TB_DEV + lax.dynamic_slice_in_dim(target_block, start, ENT_DEV, 0)
        return (accum.at[goal.astype(jnp.int32)].add(made), None)
    accum = jnp.zeros((TB_DEV * N_BAND, PIX, C), jnp.float32)
    accum, unused = lax.scan(per_device, accum, jnp.arange(N_BAND, dtype=jnp.int32))
    regridded = accum.astype(jnp.bfloat16).reshape(NLAT, NLON, C)
    forward, inverse = lon_tables(mode_index)
    spectrum = jnp.einsum('lnc,nk->lkc', regridded.astype(jnp.float32), forward.astype(jnp.float32)) * (1.0 / math.sqrt(NLON))
    spectrum = spectrum.astype(jnp.bfloat16).reshape(2 * NLAT, MODES * C)
    table = lat_table(NLAT)
    mixed = jnp.dot(table, spectrum, preferred_element_type=jnp.float32) * (1.0 / math.sqrt(NLAT))
    mixed = mixed.reshape(NLAT, 2, MODES, C)
    filt = filter_weight.astype(jnp.float32)
    real_part = filt[:, 0] * mixed[:, 0] - filt[:, 1] * mixed[:, 1]
    imag_part = filt[:, 0] * mixed[:, 1] + filt[:, 1] * mixed[:, 0]
    shaped = jnp.stack([real_part, imag_part], axis=1).astype(jnp.bfloat16).reshape(2 * NLAT, MODES * C)
    back = jnp.dot(table.T, shaped, preferred_element_type=jnp.float32) * (1.0 / math.sqrt(NLAT))
    back = back.astype(jnp.bfloat16).reshape(NLAT, 2 * MODES, C)
    filtered = jnp.einsum('lkc,kn->lnc', back.astype(jnp.float32), inverse.astype(jnp.float32)) * (1.0 / math.sqrt(NLON))
    processed = (regridded.astype(jnp.float32) + filtered).astype(jnp.bfloat16)
    return processed.reshape(NLAT * NLON, C)
```

```python
import math

import jax
import jax.numpy as jnp
from jax import lax
from jax.experimental import pallas as pl
from jax.experimental.pallas import tpu as pltpu
from jax.sharding import PartitionSpec as P

NLON = 1440
LAT_DEV = 4
TB_DEV = 45
CHUNKS = 2


def lon_tables(mode_index, bands):
    grid_n = jnp.arange(NLON, dtype=jnp.int32)
    phase = grid_n[:, None] * mode_index[None, :] % NLON
    angle = phase.astype(jnp.float32) * (2.0 * math.pi / NLON)
    modes = mode_index.shape[0]
    factor = jnp.where((mode_index == 0) | (mode_index == NLON // 2), 1.0, 2.0).astype(jnp.float32)
    cosine = jnp.cos(angle)
    sine = jnp.sin(angle)

    def by_owner(a, b):
        both = [a.reshape(NLON, bands, 1, -1), b.reshape(NLON, bands, 1, -1)]
        return jnp.concatenate(both, axis=2).reshape(NLON, 2 * modes).astype(jnp.bfloat16)

    forward = by_owner(cosine, -sine)
    inverse = by_owner(factor[None, :] * cosine, -factor[None, :] * sine)
    return forward, inverse


def lat_table(nlat):
    index = jnp.arange(nlat, dtype=jnp.int32)
    phase = index[:, None] * index[None, :] % nlat
    angle = phase.astype(jnp.float32) * (2.0 * math.pi / nlat)
    cosine = jnp.cos(angle)
    sine = jnp.sin(angle)
    upper = jnp.stack([cosine, sine], axis=2)
    lower = jnp.stack([-sine, cosine], axis=2)
    table = jnp.stack([upper, lower], axis=1)
    return table.reshape(2 * nlat, 2 * nlat).astype(jnp.bfloat16)


def make_kernel(slots, entry_ref, source_ref, weight_ref, field_ref, out_ref):
    band = pl.program_id(0)
    for slot in range(slots):
        at = band * slots + slot
        out_ref[0, slot] = jnp.dot(
            weight_ref[entry_ref[at]],
            field_ref[source_ref[at]],
            preferred_element_type=jnp.float32,
        ).astype(out_ref.dtype)


def make_contributions(entry, source, weight, field, bands, slots, part, width):
    pixels = field.shape[1]
    return pl.pallas_call(
        lambda *refs: make_kernel(slots, *refs),
        out_shape=jax.ShapeDtypeStruct((bands, slots, pixels, width), jnp.bfloat16),
        grid_spec=pltpu.PrefetchScalarGridSpec(
            num_scalar_prefetch=2,
            grid=(bands,),
            in_specs=[
                pl.BlockSpec(weight.shape, lambda b, *_: (0, 0, 0)),
                pl.BlockSpec((field.shape[0], pixels, width), lambda b, *_: (0, 0, part)),
            ],
            out_specs=pl.BlockSpec((1, slots, pixels, width), lambda b, *_: (b, 0, 0, 0)),
        ),
        compiler_params=pltpu.CompilerParams(vmem_limit_bytes=32 * 2**20),
        cost_estimate=pl.CostEstimate(
            flops=2 * bands * slots * pixels * pixels * width * 4,
            bytes_accessed=2 * bands * slots * pixels * width,
            transcendentals=0,
        ),
        name="make_contributions",
    )(entry, source, weight, field)


def regrid_kernel(bands, slots, ids_ref, arrived_ref, out_ref, total_ref):
    band = pl.program_id(0)

    @pl.when(band == 0)
    def _():
        total_ref[...] = jnp.zeros_like(total_ref)

    for slot in range(slots):
        block = ids_ref[band * slots + slot]

        @pl.when(block >= 0)
        def _():
            total_ref[block] += arrived_ref[0, slot].astype(jnp.float32)

    @pl.when(band == bands - 1)
    def _():
        out_ref[...] = total_ref[...].astype(out_ref.dtype)


def regrid(ids, arrived):
    bands, slots, pixels, width = arrived.shape
    return pl.pallas_call(
        lambda *refs: regrid_kernel(bands, slots, *refs),
        out_shape=jax.ShapeDtypeStruct((TB_DEV, pixels, width), jnp.bfloat16),
        grid_spec=pltpu.PrefetchScalarGridSpec(
            num_scalar_prefetch=1,
            grid=(bands,),
            in_specs=[pl.BlockSpec((1, slots, pixels, width), lambda b, *_: (b, 0, 0, 0))],
            out_specs=pl.BlockSpec((TB_DEV, pixels, width), lambda b, *_: (0, 0, 0)),
            scratch_shapes=[pltpu.VMEM((TB_DEV, pixels, width), jnp.float32)],
        ),
        compiler_params=pltpu.CompilerParams(vmem_limit_bytes=32 * 2**20),
        cost_estimate=pl.CostEstimate(
            flops=bands * slots * pixels * width,
            bytes_accessed=2 * bands * slots * pixels * width + 2 * TB_DEV * pixels * width,
            transcendentals=0,
        ),
        name="regrid",
    )(ids, arrived)


def per_device(
    source_field,
    interp_weight,
    dest_band,
    target_block,
    source_block,
    entry_count,
    mode_index,
    filter_weight,
):
    bands = lax.axis_size("band")
    entries = interp_weight.shape[0]
    slots = max(2, 3 * entries // (2 * bands))
    total_slots = bands * slots
    channels = source_field.shape[2]
    width = channels // CHUNKS
    modes = mode_index.shape[0]
    mode_dev = modes // bands
    nlat = LAT_DEV * bands

    entry_ids = jnp.arange(entries, dtype=jnp.int32)
    dest = dest_band[:, 0]
    valid = entry_ids < entry_count[0]

    earlier = (dest[:, None] == dest[None, :]) & (entry_ids[:, None] > entry_ids[None, :])
    rank = jnp.sum(earlier.astype(jnp.int32), axis=1)
    position = dest * slots + rank
    slot_ids = jnp.arange(total_slots, dtype=jnp.int32)
    placed = slot_ids[:, None] == position[None, :]
    entry_of = jnp.sum(jnp.where(placed, entry_ids[None, :], 0), axis=1)
    source_of = jnp.sum(jnp.where(placed, source_block[None, :], 0), axis=1)
    target_of = jnp.max(
        jnp.where(placed & valid[None, :], target_block[None, :], -1), axis=1
    ).reshape(bands, slots)

    ids = lax.all_to_all(target_of, "band", split_axis=0, concat_axis=0, tiled=True)
    ids = ids.reshape(total_slots)

    sent = []
    for part in range(CHUNKS):
        made = make_contributions(
            entry_of, source_of, interp_weight, source_field, bands, slots, part, width
        )
        sent.append(lax.all_to_all(made, "band", split_axis=0, concat_axis=0, tiled=True))

    forward, inverse = lon_tables(mode_index, bands)
    table = lat_table(nlat)
    filt = filter_weight.astype(jnp.float32)
    grids, returned = [], []
    for part in range(CHUNKS):
        grid = regrid(ids, sent[part]).reshape(LAT_DEV, NLON, width)
        grids.append(grid)
        spectrum = jnp.einsum(
            "lnc,nk->lkc", grid, forward, preferred_element_type=jnp.float32
        ) * (1.0 / math.sqrt(NLON))
        spectrum = spectrum.astype(jnp.bfloat16).reshape(LAT_DEV, bands, 2 * mode_dev, width)
        spectrum = spectrum.transpose(1, 0, 2, 3)
        pencils = lax.all_to_all(spectrum, "band", split_axis=0, concat_axis=0, tiled=True)
        mixed = jnp.dot(
            table,
            pencils.reshape(2 * nlat, mode_dev * width),
            preferred_element_type=jnp.float32,
        ) * (1.0 / math.sqrt(nlat))
        mixed = mixed.reshape(nlat, 2, mode_dev, width)
        own = filt[..., part * width : (part + 1) * width]
        real_part = own[:, 0] * mixed[:, 0] - own[:, 1] * mixed[:, 1]
        imag_part = own[:, 0] * mixed[:, 1] + own[:, 1] * mixed[:, 0]
        shaped = (
            jnp.stack([real_part, imag_part], axis=1)
            .astype(jnp.bfloat16)
            .reshape(2 * nlat, mode_dev * width)
        )
        back = lax.dot_general(
            table, shaped, (((0,), (0,)), ((), ())), preferred_element_type=jnp.float32
        ) * (1.0 / math.sqrt(nlat))
        back = back.astype(jnp.bfloat16).reshape(bands, LAT_DEV, 2 * mode_dev, width)
        back = lax.all_to_all(back, "band", split_axis=0, concat_axis=0, tiled=True)
        returned.append(back.transpose(1, 0, 2, 3).reshape(LAT_DEV, 2 * modes, width))

    filtered = jnp.einsum(
        "lkc,nk->lnc",
        jnp.concatenate(returned, axis=2),
        inverse,
        preferred_element_type=jnp.float32,
    ) * (1.0 / math.sqrt(NLON))
    regridded = jnp.concatenate(grids, axis=2)
    processed = (regridded.astype(jnp.float32) + filtered).astype(jnp.bfloat16)
    return processed.reshape(LAT_DEV * NLON, channels)


def solution(mesh):
    in_specs = (
        P(("grp", "band"), None, None),
        P("band", None, None),
        P("band", None),
        P("band"),
        P("band"),
        P("band"),
        P(),
        P(None, None, "band", None),
    )
    out_specs = P(("grp", "band"), None)
    return jax.shard_map(
        per_device, mesh=mesh, in_specs=in_specs, out_specs=out_specs, check_vma=False
    )
```

```python
import math

import jax
import jax.numpy as jnp
from jax import lax
from jax.experimental import pallas as pl
from jax.experimental.pallas import tpu as pltpu
from jax.sharding import PartitionSpec as P

NLON = 1440
LAT_DEV = 4
TB_DEV = 45
CHUNKS = 2


def lon_table(mode_index, bands, rows):
    step = 36
    high = jnp.arange(0, NLON, step, dtype=jnp.int32)
    low = jnp.arange(step, dtype=jnp.int32)

    def waves(index):
        phase = mode_index[:, None] * index[None, :] % NLON
        angle = phase.astype(jnp.float32) * (2.0 * math.pi / NLON)
        return jnp.cos(angle), jnp.sin(angle)

    cos_high, sin_high = [w[:, :, None] for w in waves(high)]
    cos_low, sin_low = [w[:, None, :] for w in waves(low)]
    modes = mode_index.shape[0]
    cosine = (cos_high * cos_low - sin_high * sin_low).reshape(bands, 1, modes // bands, NLON)
    sine = (sin_high * cos_low + cos_high * sin_low).reshape(bands, 1, modes // bands, NLON)
    forward = jnp.concatenate([cosine, -sine], axis=1).astype(jnp.bfloat16)
    forward = forward.reshape(bands, 2 * (modes // bands), NLON)
    forward = jnp.pad(forward, ((0, 0), (0, rows - forward.shape[1]), (0, 0)))
    return forward.reshape(bands * rows, NLON)


def lat_table(nlat):
    index = jnp.arange(nlat, dtype=jnp.int32)
    phase = index[:, None] * index[None, :] % nlat
    angle = phase.astype(jnp.float32) * (2.0 * math.pi / nlat)
    cosine = jnp.cos(angle)
    sine = jnp.sin(angle)
    upper = jnp.stack([cosine, sine], axis=2)
    lower = jnp.stack([-sine, cosine], axis=2)
    table = jnp.stack([upper, lower], axis=1)
    return table.reshape(2 * nlat, 2 * nlat).astype(jnp.bfloat16)


def spectra_kernel(
    bands,
    slots,
    entry_ref,
    source_ref,
    order_ref,
    keep_ref,
    last_ref,
    has_ref,
    weight_ref,
    field_ref,
    table_ref,
    grid_ref,
    spectra_ref,
    send_ref,
    recv_a_ref,
    recv_b_ref,
    sums_ref,
    out_ref,
    send_sem,
    recv_sem,
    out_sem,
    in_sem,
):
    me = lax.axis_index("band")
    recv_refs = (recv_a_ref, recv_b_ref)
    width = recv_a_ref.shape[-1]
    pixels = recv_a_ref.shape[-2]
    rows = spectra_ref.shape[-2]
    scale = 1.0 / math.sqrt(NLON)

    def partner(k):
        return lax.rem(me + bands // 2 + (k // 2) * (1 - 2 * lax.rem(k, 2)), bands)

    def block_copy(part, other, slot):
        return pltpu.make_async_remote_copy(
            src_ref=send_ref.at[part, other],
            dst_ref=recv_refs[part].at[slot],
            send_sem=send_sem.at[part, other],
            recv_sem=recv_sem.at[part, slot],
            device_id={"band": other},
            device_id_type=pl.DeviceIdType.MESH,
        )

    def spectrum_copy(part, other, slot):
        return pltpu.make_async_remote_copy(
            src_ref=out_ref.at[part, other],
            dst_ref=spectra_ref.at[part, slot],
            send_sem=out_sem.at[part, other],
            recv_sem=in_sem.at[part, slot],
            device_id={"band": other},
            device_id_type=pl.DeviceIdType.MESH,
        )

    def loop(body):
        def step(k, carry):
            body(partner(k))
            return carry

        lax.fori_loop(1, bands, step, 0)

    barrier = pltpu.get_barrier_semaphore()
    loop(
        lambda other: pl.semaphore_signal(
            barrier, inc=1, device_id={"band": other}, device_id_type=pl.DeviceIdType.MESH
        )
    )

    def product(part, other, slot):
        at = other * slots + slot
        block = field_ref[source_ref[at]][:, part * width : (part + 1) * width]
        return jnp.dot(
            weight_ref[entry_ref[at]], block, preferred_element_type=jnp.float32
        ).astype(jnp.bfloat16)

    pl.semaphore_wait(barrier, bands - 1)
    for part in range(CHUNKS):

        def make(other):
            for slot in range(slots):
                send_ref[part, other, slot] = product(part, other, slot)
            block_copy(part, other, me).start()

        loop(make)
        for slot in range(slots):
            recv_refs[part][me, slot] = product(part, me, slot)

    for part in range(CHUNKS):
        lanes = slice(part * width, (part + 1) * width)
        loop(lambda other: block_copy(part, other, other).wait_recv())

        def add(j, run):
            at = order_ref[j]
            run = run * keep_ref[j] + recv_refs[part][at // slots, lax.rem(at, slots)].astype(
                jnp.float32
            )
            sums_ref[part, j] = run.astype(jnp.bfloat16)
            return run

        lax.fori_loop(0, bands * slots, add, jnp.zeros((pixels, width), jnp.float32))

        def place(t, carry):
            block = sums_ref[part, last_ref[t]].astype(jnp.float32) * has_ref[t]
            start = pl.multiple_of(t * pixels, pixels)
            grid_ref[pl.ds(start, pixels), lanes] = block.astype(jnp.bfloat16)
            return carry

        lax.fori_loop(0, TB_DEV, place, 0)
        for lat in range(LAT_DEV):
            spectrum = jnp.dot(
                table_ref[...],
                grid_ref[lat * NLON : (lat + 1) * NLON, lanes],
                preferred_element_type=jnp.float32,
            )
            spectrum = (spectrum * scale).astype(jnp.bfloat16)
            out_ref[part, :, lat] = spectrum.reshape(bands, rows, width)
        loop(lambda other: spectrum_copy(part, other, me).start())
        spectra_ref[part, me] = out_ref[part, me]

    for part in range(CHUNKS):
        loop(lambda other: spectrum_copy(part, other, other).wait_recv())
        loop(lambda other: spectrum_copy(part, other, me).wait_send())
        loop(lambda other: block_copy(part, other, me).wait_send())


def spectra_of_bands(scalars, weight, field, table, bands, slots, rows):
    pixels = field.shape[1]
    width = field.shape[2] // CHUNKS
    blocks = (CHUNKS, bands, slots, pixels, width)
    spectra = (CHUNKS, bands, LAT_DEV, rows, width)
    smem = pl.BlockSpec(memory_space=pltpu.SMEM)
    vmem = pl.BlockSpec(memory_space=pltpu.VMEM)
    dma = pltpu.SemaphoreType.DMA((CHUNKS, bands))
    return pl.pallas_call(
        lambda *refs: spectra_kernel(bands, slots, *refs),
        out_shape=(
            jax.ShapeDtypeStruct((LAT_DEV * NLON, field.shape[2]), jnp.bfloat16),
            jax.ShapeDtypeStruct(spectra, jnp.bfloat16),
        ),
        in_specs=[smem] * len(scalars) + [vmem] * 3,
        out_specs=(vmem, vmem),
        scratch_shapes=[
            pltpu.VMEM(blocks, jnp.bfloat16),
            pltpu.VMEM(blocks[1:], jnp.bfloat16),
            pltpu.VMEM(blocks[1:], jnp.bfloat16),
            pltpu.VMEM((CHUNKS, bands * slots, pixels, width), jnp.bfloat16),
            pltpu.VMEM(spectra, jnp.bfloat16),
            dma,
            dma,
            dma,
            dma,
        ],
        compiler_params=pltpu.CompilerParams(
            collective_id=0, has_side_effects=True, vmem_limit_bytes=56 * 2**20
        ),
        name="spectra_of_bands",
    )(*scalars, weight, field, table)


def per_device(
    source_field,
    interp_weight,
    dest_band,
    target_block,
    source_block,
    entry_count,
    mode_index,
    filter_weight,
):
    bands = lax.axis_size("band")
    entries = interp_weight.shape[0]
    slots = max(2, 3 * entries // (2 * bands))
    total_slots = bands * slots
    channels = source_field.shape[2]
    width = channels // CHUNKS
    modes = mode_index.shape[0]
    mode_dev = modes // bands
    nlat = LAT_DEV * bands

    entry_ids = jnp.arange(entries, dtype=jnp.int32)
    dest = dest_band[:, 0]
    valid = entry_ids < entry_count[0]

    earlier = (dest[:, None] == dest[None, :]) & (entry_ids[:, None] > entry_ids[None, :])
    rank = jnp.sum(earlier.astype(jnp.int32), axis=1)
    position = dest * slots + rank
    slot_ids = jnp.arange(total_slots, dtype=jnp.int32)
    placed = slot_ids[:, None] == position[None, :]
    entry_of = jnp.sum(jnp.where(placed, entry_ids[None, :], 0), axis=1)
    source_of = jnp.sum(jnp.where(placed, source_block[None, :], 0), axis=1)
    target_of = jnp.max(
        jnp.where(placed & valid[None, :], target_block[None, :], -1), axis=1
    ).reshape(bands, slots)

    ids = lax.all_to_all(target_of, "band", split_axis=0, concat_axis=0, tiled=True)
    ids = ids.reshape(total_slots)
    ids = jnp.where(ids < 0, TB_DEV, ids)
    keys = ids * total_slots + slot_ids
    rank = jnp.sum((keys[None, :] < keys[:, None]).astype(jnp.int32), axis=1)
    at_rank = rank[None, :] == slot_ids[:, None]
    order = jnp.sum(jnp.where(at_rank, slot_ids[None, :], 0), axis=1)
    before = jnp.sum((rank[None, :] + 1 == slot_ids[:, None]) * (ids + 1)[None, :], axis=1)
    here = jnp.sum(jnp.where(at_rank, (ids + 1)[None, :], 0), axis=1)
    keep = (before == here).astype(jnp.float32)
    blocks = jnp.arange(TB_DEV, dtype=jnp.int32)
    last = jnp.maximum(jnp.sum((ids[None, :] <= blocks[:, None]).astype(jnp.int32), axis=1) - 1, 0)
    has = jnp.max((ids[None, :] == blocks[:, None]).astype(jnp.float32), axis=1)

    rows = -(-2 * mode_dev // 16) * 16
    forward = lon_table(mode_index, bands, rows)
    scalars = (entry_of, source_of, order, keep, last, has)
    regridded, spectra = spectra_of_bands(
        scalars, interp_weight, source_field, forward, bands, slots, rows
    )

    pencils = spectra.reshape(CHUNKS, nlat, rows, width)[:, :, : 2 * mode_dev]
    pencils = pencils.reshape(CHUNKS, 2 * nlat, mode_dev, width)
    table = lat_table(nlat)
    filt = filter_weight.astype(jnp.float32)
    factor = jnp.where((mode_index == 0) | (mode_index == NLON // 2), 1.0, 2.0).astype(jnp.float32)
    factor = lax.dynamic_slice_in_dim(factor, lax.axis_index("band") * mode_dev, mode_dev)
    mixed = jnp.einsum(
        "ab,hbmc->amhc", table, pencils, preferred_element_type=jnp.float32
    ) * (1.0 / math.sqrt(nlat))
    mixed = mixed.reshape(nlat, 2, mode_dev, channels)
    real_part = filt[:, 0] * mixed[:, 0] - filt[:, 1] * mixed[:, 1]
    imag_part = filt[:, 0] * mixed[:, 1] + filt[:, 1] * mixed[:, 0]
    shaped = (
        jnp.stack([real_part, imag_part], axis=1)
        .astype(jnp.bfloat16)
        .reshape(2 * nlat, mode_dev * channels)
    )
    back = lax.dot_general(
        table, shaped, (((0,), (0,)), ((), ())), preferred_element_type=jnp.float32
    ) * (1.0 / math.sqrt(nlat))
    back = back.reshape(nlat, 2, mode_dev, channels) * factor[None, None, :, None]
    back = back.astype(jnp.bfloat16).reshape(bands, LAT_DEV, 2 * mode_dev, channels)
    back = lax.all_to_all(back, "band", split_axis=0, concat_axis=0, tiled=True)
    returned = back.transpose(1, 0, 2, 3).reshape(LAT_DEV, 2 * modes, channels)
    inverse = forward.reshape(bands, rows, NLON)[:, : 2 * mode_dev].reshape(2 * modes, NLON)
    filtered = jnp.einsum(
        "lkc,kn->lnc", returned, inverse, preferred_element_type=jnp.float32
    ) * (1.0 / math.sqrt(NLON))
    regridded = regridded.reshape(LAT_DEV, NLON, channels)
    processed = (regridded.astype(jnp.float32) + filtered).astype(jnp.bfloat16)
    return processed.reshape(LAT_DEV * NLON, channels)


def solution(mesh):
    in_specs = (
        P(("grp", "band"), None, None),
        P("band", None, None),
        P("band", None),
        P("band"),
        P("band"),
        P("band"),
        P(),
        P(None, None, "band", None),
    )
    out_specs = P(("grp", "band"), None)
    return jax.shard_map(
        per_device, mesh=mesh, in_specs=in_specs, out_specs=out_specs, check_vma=False
    )
```

```python
import math

import jax
import jax.numpy as jnp
from jax import lax
from jax.experimental import pallas as pl
from jax.experimental.pallas import tpu as pltpu
from jax.sharding import PartitionSpec as P

NLON = 1440
LAT_DEV = 4
TB_DEV = 45
CHUNKS = 2
LANES = 128
ROW_STEP = 32
GROUP = 6


def waves(phase, period):
    angle = (phase % period).astype(jnp.float32) * (2.0 * math.pi / period)
    return jnp.cos(angle), jnp.sin(angle)


def lon_parts(mode_index, bands, rows):
    per_band = mode_index.shape[0] // bands
    mode = jnp.broadcast_to(mode_index.reshape(bands, 1, per_band), (bands, 2, per_band))
    mode = mode.reshape(bands, 2 * per_band)
    mode = jnp.pad(mode, ((0, 0), (0, rows - 2 * per_band))).reshape(bands * rows)
    real = jnp.arange(bands * rows, dtype=jnp.int32) % rows < per_band
    outs = []
    for step, along in ((LANES, 1), (ROW_STEP, 0)):
        high = jnp.arange(0, NLON, step, dtype=jnp.int32)
        low = jnp.arange(step, dtype=jnp.int32)
        pick = jnp.expand_dims(real, along)
        modes = jnp.expand_dims(mode, along)
        cos_high, sin_high = waves(modes * jnp.expand_dims(high, 1 - along), NLON)
        cos_low, sin_low = waves(modes * jnp.expand_dims(low, 1 - along), NLON)
        outer = jnp.where(pick, cos_high, -sin_high)
        inner = jnp.where(pick, -sin_high, -cos_high)
        outs += [outer, inner, cos_low, sin_low]
    return outs


def lat_tables(nlat):
    index = jnp.arange(nlat, dtype=jnp.int32)
    cosine, sine = waves(index[:, None] * index[None, :], nlat)
    upper = jnp.concatenate([cosine, sine], axis=1)
    lower = jnp.concatenate([-sine, cosine], axis=1)
    turned = jnp.concatenate([cosine, -sine], axis=1)
    table = jnp.concatenate([upper, lower], axis=0).astype(jnp.bfloat16)
    flipped = jnp.concatenate(
        [turned, jnp.concatenate([sine, cosine], axis=1)], axis=0
    ).astype(jnp.bfloat16)
    return table, flipped


def layer_kernel(
    bands,
    slots,
    entry_ref,
    source_ref,
    order_ref,
    keep_ref,
    last_ref,
    has_ref,
    factor_ref,
    weight_ref,
    field_ref,
    filter_ref,
    outer_ref,
    inner_ref,
    cos_low_ref,
    sin_low_ref,
    outer_row_ref,
    inner_row_ref,
    cos_row_ref,
    sin_row_ref,
    lat_ref,
    lat_flipped_ref,
    out_ref,
    send_a_ref,
    send_b_ref,
    recv_a_ref,
    recv_b_ref,
    table_ref,
    inverse_ref,
    filter_f32_ref,
    spec_send_ref,
    spec_recv_ref,
    back_send_ref,
    back_recv_ref,
    mode_ref,
    shaped_ref,
    send_sem,
    recv_sem,
    spec_send_sem,
    spec_recv_sem,
    back_send_sem,
    back_recv_sem,
):
    me = lax.axis_index("band")
    send_refs = (send_a_ref, send_b_ref)
    recv_refs = (recv_a_ref, recv_b_ref)
    width = recv_a_ref.shape[-1]
    pixels = recv_a_ref.shape[-2]
    rows = spec_recv_ref.shape[-2]
    nlat = LAT_DEV * bands
    mode_dev = filter_ref.shape[2]
    filter_total = filter_f32_ref.shape[0] // CHUNKS
    filter_rows = filter_total // (2 * nlat)
    lon_scale = 1.0 / math.sqrt(NLON)
    lat_scale = 1.0 / math.sqrt(nlat)

    def partner(k):
        return lax.rem(me + bands // 2 + (k // 2) * (1 - 2 * lax.rem(k, 2)), bands)

    def remote(source, goal, out_sem, in_sem, part, other, slot):
        return pltpu.make_async_remote_copy(
            src_ref=source.at[other],
            dst_ref=goal.at[slot],
            send_sem=out_sem.at[part, other],
            recv_sem=in_sem.at[part, slot],
            device_id={"band": other},
            device_id_type=pl.DeviceIdType.MESH,
        )

    def block_copy(part, other, slot):
        return remote(send_refs[part], recv_refs[part], send_sem, recv_sem, part, other, slot)

    def spectrum_copy(part, other, slot):
        return remote(
            spec_send_ref.at[part],
            spec_recv_ref.at[part],
            spec_send_sem,
            spec_recv_sem,
            part,
            other,
            slot,
        )

    def back_copy(part, other, slot):
        return remote(
            back_send_ref.at[part],
            back_recv_ref.at[part],
            back_send_sem,
            back_recv_sem,
            part,
            other,
            slot,
        )

    def loop(body):
        def step(k, carry):
            body(partner(k))
            return carry

        lax.fori_loop(1, bands, step, 0)

    barrier = pltpu.get_barrier_semaphore()
    loop(
        lambda other: pl.semaphore_signal(
            barrier, inc=1, device_id={"band": other}, device_id_type=pl.DeviceIdType.MESH
        )
    )

    def product(part, other, slot):
        at = other * slots + slot
        block = field_ref[source_ref[at]][:, part * width : (part + 1) * width]
        return jnp.dot(
            weight_ref[entry_ref[at]], block, preferred_element_type=jnp.float32
        ).astype(jnp.bfloat16)

    pl.semaphore_wait(barrier, bands - 1)
    for part in range(CHUNKS):

        def make(other):
            for slot in range(slots):
                send_refs[part][other, slot] = product(part, other, slot)
            block_copy(part, other, me).start()

        loop(make)
        for slot in range(slots):
            recv_refs[part][me, slot] = product(part, me, slot)

    for first in range(0, NLON, LANES):
        span = min(LANES, NLON - first)
        at = first // LANES
        table_ref[:, first : first + span] = (
            outer_ref[:, at : at + 1] * cos_low_ref[:, :span]
            + inner_ref[:, at : at + 1] * sin_low_ref[:, :span]
        ).astype(jnp.bfloat16)
    for first in range(0, NLON, ROW_STEP):
        at = first // ROW_STEP
        inverse_ref[first : first + ROW_STEP, :] = (
            outer_row_ref[at : at + 1, :] * cos_row_ref[...]
            + inner_row_ref[at : at + 1, :] * sin_row_ref[...]
        ).astype(jnp.bfloat16)

    def widen(lat, carry):
        for half in range(2):
            start = pl.multiple_of((lat * 2 + half) * filter_rows, 8)
            block = filter_ref[lat, half].astype(jnp.float32)
            for part in range(CHUNKS):
                filter_f32_ref[pl.ds(part * filter_total + start, mode_dev), :] = block[
                    :, part * width : (part + 1) * width
                ]
        return carry

    lax.fori_loop(0, nlat, widen, 0)
    if rows > 2 * mode_dev:
        shaped_ref[...] = jnp.zeros_like(shaped_ref)

    for part in range(CHUNKS):
        lanes = slice(part * width, (part + 1) * width)
        sums_ref = send_refs[part]
        loop(lambda other: block_copy(part, other, other).wait_recv())
        loop(lambda other: block_copy(part, other, me).wait_send())

        def add(j, run):
            at = order_ref[j]
            run = run * keep_ref[j] + recv_refs[part][at // slots, lax.rem(at, slots)].astype(
                jnp.float32
            )
            sums_ref[j // slots, lax.rem(j, slots)] = run.astype(jnp.bfloat16)
            return run

        lax.fori_loop(0, bands * slots, add, jnp.zeros((pixels, width), jnp.float32))

        def place(t, carry):
            at = last_ref[t]
            block = sums_ref[at // slots, lax.rem(at, slots)].astype(jnp.float32) * has_ref[t]
            start = pl.multiple_of(t * pixels, pixels)
            out_ref[pl.ds(start, pixels), lanes] = block.astype(jnp.bfloat16)
            return carry

        lax.fori_loop(0, TB_DEV, place, 0)
        for lat in range(LAT_DEV):
            spectrum = jnp.dot(
                table_ref[...],
                out_ref[lat * NLON : (lat + 1) * NLON, lanes],
                preferred_element_type=jnp.float32,
            )
            spectrum = (spectrum * lon_scale).astype(jnp.bfloat16)
            spec_send_ref[part, :, lat] = spectrum.reshape(bands, rows, width)
        loop(lambda other: spectrum_copy(part, other, me).start())
        spec_recv_ref[part, me] = spec_send_ref[part, me]

    for part in range(CHUNKS):
        loop(lambda other: spectrum_copy(part, other, other).wait_recv())

        def spread(band, carry):
            start = pl.multiple_of(band * LAT_DEV * rows, LAT_DEV * rows)
            block = spec_recv_ref[part, band].astype(jnp.float32)
            mode_ref[pl.ds(start, LAT_DEV * rows), :] = block.reshape(LAT_DEV * rows, width)
            return carry

        lax.fori_loop(0, bands, spread, 0)

        def mix(group, carry):
            columns = []
            for i in range(GROUP):
                mode = group * GROUP + i
                halves = [
                    mode_ref[pl.ds(half * mode_dev + mode, nlat, stride=rows), :]
                    for half in range(2)
                ]
                columns.append(jnp.concatenate(halves, axis=0).astype(jnp.bfloat16))
            mixed = (
                jnp.dot(
                    lat_ref[...],
                    jnp.concatenate(columns, axis=1),
                    preferred_element_type=jnp.float32,
                )
                * lat_scale
            )
            columns = []
            for i in range(GROUP):
                mode = group * GROUP + i
                own = mixed[:, i * width : (i + 1) * width]
                gain = [
                    filter_f32_ref[
                        pl.ds(
                            part * filter_total + half * filter_rows + mode,
                            nlat,
                            stride=2 * filter_rows,
                        ),
                        :,
                    ]
                    for half in range(2)
                ]
                real, imag = own[:nlat], own[nlat:]
                shaped = jnp.concatenate(
                    [gain[0] * real - gain[1] * imag, gain[0] * imag + gain[1] * real], axis=0
                )
                columns.append(shaped.astype(jnp.bfloat16))
            back = (
                jnp.dot(
                    lat_flipped_ref[...],
                    jnp.concatenate(columns, axis=1),
                    preferred_element_type=jnp.float32,
                )
                * lat_scale
            )
            for i in range(GROUP):
                mode = group * GROUP + i
                own = back[:, i * width : (i + 1) * width] * factor_ref[mode]
                for half in range(2):
                    shaped_ref[pl.ds(half * mode_dev + mode, nlat, stride=rows), :] = own[
                        half * nlat : (half + 1) * nlat
                    ]
            return carry

        lax.fori_loop(0, mode_dev // GROUP, mix, 0)

        def back_block(band):
            start = pl.multiple_of(band * LAT_DEV * rows, LAT_DEV * rows)
            block = shaped_ref[pl.ds(start, LAT_DEV * rows), :].astype(jnp.bfloat16)
            return block.reshape(LAT_DEV, rows, width)

        def give_back(other):
            back_send_ref[part, other] = back_block(other)
            back_copy(part, other, me).start()

        loop(give_back)
        back_recv_ref[part, me] = back_block(me)

    for part in range(CHUNKS):
        lanes = slice(part * width, (part + 1) * width)
        loop(lambda other: back_copy(part, other, other).wait_recv())
        for lat in range(LAT_DEV):
            filtered = jnp.dot(
                inverse_ref[...],
                back_recv_ref[part, :, lat].reshape(bands * rows, width),
                preferred_element_type=jnp.float32,
            )
            span = slice(lat * NLON, (lat + 1) * NLON)
            out_ref[span, lanes] = (
                out_ref[span, lanes].astype(jnp.float32) + filtered * lon_scale
            ).astype(jnp.bfloat16)
        loop(lambda other: spectrum_copy(part, other, me).wait_send())
        loop(lambda other: back_copy(part, other, me).wait_send())


def layer(scalars, tensors, bands, slots, rows):
    field, filters = tensors[1], tensors[2]
    pixels = field.shape[1]
    width = field.shape[2] // CHUNKS
    nlat, _, mode_dev, channels = filters.shape
    blocks = pltpu.VMEM((bands, slots, pixels, width), jnp.bfloat16)
    spectra = pltpu.VMEM((CHUNKS, bands, LAT_DEV, rows, width), jnp.bfloat16)
    filter_rows = -(-mode_dev // 8) * 8
    smem = pl.BlockSpec(memory_space=pltpu.SMEM)
    vmem = pl.BlockSpec(memory_space=pltpu.VMEM)
    return pl.pallas_call(
        lambda *refs: layer_kernel(bands, slots, *refs),
        out_shape=jax.ShapeDtypeStruct((LAT_DEV * NLON, channels), jnp.bfloat16),
        in_specs=[smem] * len(scalars) + [vmem] * len(tensors),
        out_specs=vmem,
        scratch_shapes=[
            blocks,
            blocks,
            blocks,
            blocks,
            pltpu.VMEM((bands * rows, NLON), jnp.bfloat16),
            pltpu.VMEM((NLON, bands * rows), jnp.bfloat16),
            pltpu.VMEM((CHUNKS * nlat * 2 * filter_rows, width), jnp.float32),
            spectra,
            spectra,
            spectra,
            spectra,
            pltpu.VMEM((nlat * rows, width), jnp.float32),
            pltpu.VMEM((nlat * rows, width), jnp.float32),
        ]
        + [pltpu.SemaphoreType.DMA((CHUNKS, bands))] * 6,
        compiler_params=pltpu.CompilerParams(
            collective_id=0, has_side_effects=True, vmem_limit_bytes=60 * 2**20
        ),
        name="layer",
    )(*scalars, *tensors)


def per_device(
    source_field,
    interp_weight,
    dest_band,
    target_block,
    source_block,
    entry_count,
    mode_index,
    filter_weight,
):
    bands = lax.axis_size("band")
    entries = interp_weight.shape[0]
    slots = max(2, 3 * entries // (2 * bands))
    total_slots = bands * slots
    mode_dev = mode_index.shape[0] // bands
    nlat = LAT_DEV * bands

    entry_ids = jnp.arange(entries, dtype=jnp.int32)
    dest = dest_band[:, 0]
    valid = entry_ids < entry_count[0]

    earlier = (dest[:, None] == dest[None, :]) & (entry_ids[:, None] > entry_ids[None, :])
    rank = jnp.sum(earlier.astype(jnp.int32), axis=1)
    position = dest * slots + rank
    slot_ids = jnp.arange(total_slots, dtype=jnp.int32)
    placed = slot_ids[:, None] == position[None, :]
    entry_of = jnp.sum(jnp.where(placed, entry_ids[None, :], 0), axis=1)
    source_of = jnp.sum(jnp.where(placed, source_block[None, :], 0), axis=1)
    target_of = jnp.max(
        jnp.where(placed & valid[None, :], target_block[None, :], -1), axis=1
    ).reshape(bands, slots)

    ids = lax.all_to_all(target_of, "band", split_axis=0, concat_axis=0, tiled=True)
    ids = ids.reshape(total_slots)
    ids = jnp.where(ids < 0, TB_DEV, ids)
    keys = ids * total_slots + slot_ids
    rank = jnp.sum((keys[None, :] < keys[:, None]).astype(jnp.int32), axis=1)
    at_rank = rank[None, :] == slot_ids[:, None]
    order = jnp.sum(jnp.where(at_rank, slot_ids[None, :], 0), axis=1)
    before = jnp.sum((rank[None, :] + 1 == slot_ids[:, None]) * (ids + 1)[None, :], axis=1)
    here = jnp.sum(jnp.where(at_rank, (ids + 1)[None, :], 0), axis=1)
    keep = (before == here).astype(jnp.float32)
    blocks = jnp.arange(TB_DEV, dtype=jnp.int32)
    last = jnp.maximum(jnp.sum((ids[None, :] <= blocks[:, None]).astype(jnp.int32), axis=1) - 1, 0)
    has = jnp.max((ids[None, :] == blocks[:, None]).astype(jnp.float32), axis=1)

    rows = -(-2 * mode_dev // 16) * 16
    factor = jnp.where((mode_index == 0) | (mode_index == NLON // 2), 1.0, 2.0).astype(jnp.float32)
    factor = lax.dynamic_slice_in_dim(factor, lax.axis_index("band") * mode_dev, mode_dev)
    scalars = (entry_of, source_of, order, keep, last, has, factor)
    tensors = (
        interp_weight,
        source_field,
        filter_weight,
        *lon_parts(mode_index, bands, rows),
        *lat_tables(nlat),
    )
    return layer(scalars, tensors, bands, slots, rows)


def solution(mesh):
    in_specs = (
        P(("grp", "band"), None, None),
        P("band", None, None),
        P("band", None),
        P("band"),
        P("band"),
        P("band"),
        P(),
        P(None, None, "band", None),
    )
    out_specs = P(("grp", "band"), None)
    return jax.shard_map(
        per_device, mesh=mesh, in_specs=in_specs, out_specs=out_specs, check_vma=False
    )
```

```python
import math

import jax
import jax.numpy as jnp
from jax import lax
from jax.experimental import pallas as pl
from jax.experimental.pallas import tpu as pltpu
from jax.sharding import PartitionSpec as P

NLON = 1440
LAT_DEV = 4
TB_DEV = 45
CHUNKS = 2
LANES = 128
ROW_STEP = 32
GROUP = 6


def waves(phase, period):
    angle = (phase % period).astype(jnp.float32) * (2.0 * math.pi / period)
    return jnp.cos(angle), jnp.sin(angle)


def lon_parts(mode_index, bands, rows):
    per_band = mode_index.shape[0] // bands
    mode = jnp.broadcast_to(mode_index.reshape(bands, 1, per_band), (bands, 2, per_band))
    mode = mode.reshape(bands, 2 * per_band)
    mode = jnp.pad(mode, ((0, 0), (0, rows - 2 * per_band))).reshape(bands * rows)
    real = jnp.arange(bands * rows, dtype=jnp.int32) % rows < per_band
    outs = []
    for step, along in ((LANES, 1), (ROW_STEP, 0)):
        high = jnp.arange(0, NLON, step, dtype=jnp.int32)
        low = jnp.arange(step, dtype=jnp.int32)
        pick = jnp.expand_dims(real, along)
        modes = jnp.expand_dims(mode, along)
        cos_high, sin_high = waves(modes * jnp.expand_dims(high, 1 - along), NLON)
        cos_low, sin_low = waves(modes * jnp.expand_dims(low, 1 - along), NLON)
        outer = jnp.where(pick, cos_high, -sin_high)
        inner = jnp.where(pick, -sin_high, -cos_high)
        outs += [outer, inner, cos_low, sin_low]
    return outs


def lat_tables(nlat):
    index = jnp.arange(nlat, dtype=jnp.int32)
    cosine, sine = waves(index[:, None] * index[None, :], nlat)
    upper = jnp.concatenate([cosine, sine], axis=1)
    lower = jnp.concatenate([-sine, cosine], axis=1)
    turned = jnp.concatenate([cosine, -sine], axis=1)
    table = jnp.concatenate([upper, lower], axis=0).astype(jnp.bfloat16)
    flipped = jnp.concatenate(
        [turned, jnp.concatenate([sine, cosine], axis=1)], axis=0
    ).astype(jnp.bfloat16)
    return table, flipped


def layer_kernel(
    bands,
    slots,
    entry_ref,
    source_ref,
    order_ref,
    keep_ref,
    last_ref,
    has_ref,
    factor_ref,
    weight_ref,
    field_ref,
    filter_ref,
    outer_ref,
    inner_ref,
    cos_low_ref,
    sin_low_ref,
    outer_row_ref,
    inner_row_ref,
    cos_row_ref,
    sin_row_ref,
    lat_ref,
    lat_flipped_ref,
    out_ref,
    send_a_ref,
    send_b_ref,
    recv_a_ref,
    recv_b_ref,
    table_ref,
    inverse_ref,
    filter_f32_ref,
    spec_send_ref,
    spec_recv_ref,
    back_send_ref,
    back_recv_ref,
    mode_ref,
    shaped_ref,
    send_sem,
    recv_sem,
    spec_send_sem,
    spec_recv_sem,
    back_send_sem,
    back_recv_sem,
):
    me = lax.axis_index("band")
    send_refs = (send_a_ref, send_b_ref)
    recv_refs = (recv_a_ref, recv_b_ref)
    width = recv_a_ref.shape[-1]
    pixels = recv_a_ref.shape[-2]
    rows = spec_recv_ref.shape[-2]
    nlat = LAT_DEV * bands
    mode_dev = filter_ref.shape[2]
    filter_total = filter_f32_ref.shape[0] // CHUNKS
    filter_rows = filter_total // (2 * nlat)
    lon_scale = 1.0 / math.sqrt(NLON)
    lat_scale = 1.0 / math.sqrt(nlat)

    def partner(k):
        return lax.rem(me + bands // 2 + (k // 2) * (1 - 2 * lax.rem(k, 2)), bands)

    def remote(source, goal, out_sem, in_sem, part, other, slot):
        return pltpu.make_async_remote_copy(
            src_ref=source.at[other],
            dst_ref=goal.at[slot],
            send_sem=out_sem.at[part, other],
            recv_sem=in_sem.at[part, slot],
            device_id={"band": other},
            device_id_type=pl.DeviceIdType.MESH,
        )

    def block_copy(part, other, slot):
        return remote(send_refs[part], recv_refs[part], send_sem, recv_sem, part, other, slot)

    def spectrum_copy(part, other, slot):
        return remote(
            spec_send_ref.at[part],
            spec_recv_ref.at[part],
            spec_send_sem,
            spec_recv_sem,
            part,
            other,
            slot,
        )

    def back_copy(part, other, slot):
        return remote(
            back_send_ref.at[part],
            back_recv_ref.at[part],
            back_send_sem,
            back_recv_sem,
            part,
            other,
            slot,
        )

    def loop(body):
        def step(k, carry):
            body(partner(k))
            return carry

        lax.fori_loop(1, bands, step, 0)

    barrier = pltpu.get_barrier_semaphore()
    loop(
        lambda other: pl.semaphore_signal(
            barrier, inc=1, device_id={"band": other}, device_id_type=pl.DeviceIdType.MESH
        )
    )

    def product(part, other, slot):
        at = other * slots + slot
        block = field_ref[source_ref[at]][:, part * width : (part + 1) * width]
        return jnp.dot(
            weight_ref[entry_ref[at]], block, preferred_element_type=jnp.float32
        ).astype(jnp.bfloat16)

    pl.semaphore_wait(barrier, bands - 1)
    def make_part(part):
        def make(other):
            for slot in range(slots):
                send_refs[part][other, slot] = product(part, other, slot)
            if part > 0:
                block_copy(part - 1, other, me).wait_send()
            block_copy(part, other, me).start()

        loop(make)
        for slot in range(slots):
            recv_refs[part][me, slot] = product(part, me, slot)

    make_part(0)
    for first in range(0, NLON, LANES):
        span = min(LANES, NLON - first)
        at = first // LANES
        table_ref[:, first : first + span] = (
            outer_ref[:, at : at + 1] * cos_low_ref[:, :span]
            + inner_ref[:, at : at + 1] * sin_low_ref[:, :span]
        ).astype(jnp.bfloat16)
    for first in range(0, NLON, ROW_STEP):
        at = first // ROW_STEP
        inverse_ref[first : first + ROW_STEP, :] = (
            outer_row_ref[at : at + 1, :] * cos_row_ref[...]
            + inner_row_ref[at : at + 1, :] * sin_row_ref[...]
        ).astype(jnp.bfloat16)

    def widen(lat, carry):
        for half in range(2):
            start = pl.multiple_of((lat * 2 + half) * filter_rows, 8)
            block = filter_ref[lat, half].astype(jnp.float32)
            for part in range(CHUNKS):
                filter_f32_ref[pl.ds(part * filter_total + start, mode_dev), :] = block[
                    :, part * width : (part + 1) * width
                ]
        return carry

    lax.fori_loop(0, nlat, widen, 0)
    if rows > 2 * mode_dev:
        shaped_ref[...] = jnp.zeros_like(shaped_ref)

    for part in range(1, CHUNKS):
        make_part(part)

    def to_spectra(part):
        lanes = slice(part * width, (part + 1) * width)
        sums_ref = send_refs[part]
        loop(lambda other: block_copy(part, other, other).wait_recv())
        if part == CHUNKS - 1:
            loop(lambda other: block_copy(part, other, me).wait_send())

        def add(j, run):
            at = order_ref[j]
            run = run * keep_ref[j] + recv_refs[part][at // slots, lax.rem(at, slots)].astype(
                jnp.float32
            )
            sums_ref[j // slots, lax.rem(j, slots)] = run.astype(jnp.bfloat16)
            return run

        lax.fori_loop(0, bands * slots, add, jnp.zeros((pixels, width), jnp.float32))

        def place(t, carry):
            at = last_ref[t]
            block = sums_ref[at // slots, lax.rem(at, slots)].astype(jnp.float32) * has_ref[t]
            start = pl.multiple_of(t * pixels, pixels)
            out_ref[pl.ds(start, pixels), lanes] = block.astype(jnp.bfloat16)
            return carry

        lax.fori_loop(0, TB_DEV, place, 0)
        for lat in range(LAT_DEV):
            spectrum = jnp.dot(
                table_ref[...],
                out_ref[lat * NLON : (lat + 1) * NLON, lanes],
                preferred_element_type=jnp.float32,
            )
            spectrum = (spectrum * lon_scale).astype(jnp.bfloat16)
            spec_send_ref[part, :, lat] = spectrum.reshape(bands, rows, width)
        loop(lambda other: spectrum_copy(part, other, me).start())
        spec_recv_ref[part, me] = spec_send_ref[part, me]

    def to_back(part):
        loop(lambda other: spectrum_copy(part, other, other).wait_recv())

        def spread(band, carry):
            start = pl.multiple_of(band * LAT_DEV * rows, LAT_DEV * rows)
            block = spec_recv_ref[part, band].astype(jnp.float32)
            mode_ref[pl.ds(start, LAT_DEV * rows), :] = block.reshape(LAT_DEV * rows, width)
            return carry

        lax.fori_loop(0, bands, spread, 0)

        def mix(group, carry):
            columns = []
            for i in range(GROUP):
                mode = group * GROUP + i
                halves = [
                    mode_ref[pl.ds(half * mode_dev + mode, nlat, stride=rows), :]
                    for half in range(2)
                ]
                columns.append(jnp.concatenate(halves, axis=0).astype(jnp.bfloat16))
            mixed = (
                jnp.dot(
                    lat_ref[...],
                    jnp.concatenate(columns, axis=1),
                    preferred_element_type=jnp.float32,
                )
                * lat_scale
            )
            columns = []
            for i in range(GROUP):
                mode = group * GROUP + i
                own = mixed[:, i * width : (i + 1) * width]
                gain = [
                    filter_f32_ref[
                        pl.ds(
                            part * filter_total + half * filter_rows + mode,
                            nlat,
                            stride=2 * filter_rows,
                        ),
                        :,
                    ]
                    for half in range(2)
                ]
                real, imag = own[:nlat], own[nlat:]
                shaped = jnp.concatenate(
                    [gain[0] * real - gain[1] * imag, gain[0] * imag + gain[1] * real], axis=0
                )
                columns.append(shaped.astype(jnp.bfloat16))
            back = (
                jnp.dot(
                    lat_flipped_ref[...],
                    jnp.concatenate(columns, axis=1),
                    preferred_element_type=jnp.float32,
                )
                * lat_scale
            )
            for i in range(GROUP):
                mode = group * GROUP + i
                own = back[:, i * width : (i + 1) * width] * factor_ref[mode]
                for half in range(2):
                    shaped_ref[pl.ds(half * mode_dev + mode, nlat, stride=rows), :] = own[
                        half * nlat : (half + 1) * nlat
                    ]
            return carry

        lax.fori_loop(0, mode_dev // GROUP, mix, 0)

        def back_block(band):
            start = pl.multiple_of(band * LAT_DEV * rows, LAT_DEV * rows)
            block = shaped_ref[pl.ds(start, LAT_DEV * rows), :].astype(jnp.bfloat16)
            return block.reshape(LAT_DEV, rows, width)

        def give_back(other):
            back_send_ref[part, other] = back_block(other)
            back_copy(part, other, me).start()

        loop(give_back)
        back_recv_ref[part, me] = back_block(me)

    def to_grid(part):
        lanes = slice(part * width, (part + 1) * width)
        loop(lambda other: back_copy(part, other, other).wait_recv())
        for lat in range(LAT_DEV):
            filtered = jnp.dot(
                inverse_ref[...],
                back_recv_ref[part, :, lat].reshape(bands * rows, width),
                preferred_element_type=jnp.float32,
            )
            span = slice(lat * NLON, (lat + 1) * NLON)
            out_ref[span, lanes] = (
                out_ref[span, lanes].astype(jnp.float32) + filtered * lon_scale
            ).astype(jnp.bfloat16)
        loop(lambda other: spectrum_copy(part, other, me).wait_send())
        loop(lambda other: back_copy(part, other, me).wait_send())

    to_spectra(0)
    for part in range(1, CHUNKS):
        to_back(part - 1)
        to_spectra(part)
        to_grid(part - 1)
    to_back(CHUNKS - 1)
    to_grid(CHUNKS - 1)


def layer(scalars, tensors, bands, slots, rows):
    field, filters = tensors[1], tensors[2]
    pixels = field.shape[1]
    width = field.shape[2] // CHUNKS
    nlat, _, mode_dev, channels = filters.shape
    blocks = pltpu.VMEM((bands, slots, pixels, width), jnp.bfloat16)
    spectra = pltpu.VMEM((CHUNKS, bands, LAT_DEV, rows, width), jnp.bfloat16)
    filter_rows = -(-mode_dev // 8) * 8
    smem = pl.BlockSpec(memory_space=pltpu.SMEM)
    vmem = pl.BlockSpec(memory_space=pltpu.VMEM)
    return pl.pallas_call(
        lambda *refs: layer_kernel(bands, slots, *refs),
        out_shape=jax.ShapeDtypeStruct((LAT_DEV * NLON, channels), jnp.bfloat16),
        in_specs=[smem] * len(scalars) + [vmem] * len(tensors),
        out_specs=vmem,
        scratch_shapes=[
            blocks,
            blocks,
            blocks,
            blocks,
            pltpu.VMEM((bands * rows, NLON), jnp.bfloat16),
            pltpu.VMEM((NLON, bands * rows), jnp.bfloat16),
            pltpu.VMEM((CHUNKS * nlat * 2 * filter_rows, width), jnp.float32),
            spectra,
            spectra,
            spectra,
            spectra,
            pltpu.VMEM((nlat * rows, width), jnp.float32),
            pltpu.VMEM((nlat * rows, width), jnp.float32),
        ]
        + [pltpu.SemaphoreType.DMA((CHUNKS, bands))] * 6,
        compiler_params=pltpu.CompilerParams(
            collective_id=0, has_side_effects=True, vmem_limit_bytes=60 * 2**20
        ),
        name="layer",
    )(*scalars, *tensors)


def per_device(
    source_field,
    interp_weight,
    dest_band,
    target_block,
    source_block,
    entry_count,
    mode_index,
    filter_weight,
):
    bands = lax.axis_size("band")
    entries = interp_weight.shape[0]
    slots = max(2, 3 * entries // (2 * bands))
    total_slots = bands * slots
    mode_dev = mode_index.shape[0] // bands
    nlat = LAT_DEV * bands

    entry_ids = jnp.arange(entries, dtype=jnp.int32)
    dest = dest_band[:, 0]
    valid = entry_ids < entry_count[0]

    earlier = (dest[:, None] == dest[None, :]) & (entry_ids[:, None] > entry_ids[None, :])
    rank = jnp.sum(earlier.astype(jnp.int32), axis=1)
    position = dest * slots + rank
    slot_ids = jnp.arange(total_slots, dtype=jnp.int32)
    placed = slot_ids[:, None] == position[None, :]
    entry_of = jnp.sum(jnp.where(placed, entry_ids[None, :], 0), axis=1)
    source_of = jnp.sum(jnp.where(placed, source_block[None, :], 0), axis=1)
    target_of = jnp.max(
        jnp.where(placed & valid[None, :], target_block[None, :], -1), axis=1
    ).reshape(bands, slots)

    ids = lax.all_to_all(target_of, "band", split_axis=0, concat_axis=0, tiled=True)
    ids = ids.reshape(total_slots)
    ids = jnp.where(ids < 0, TB_DEV, ids)
    keys = ids * total_slots + slot_ids
    rank = jnp.sum((keys[None, :] < keys[:, None]).astype(jnp.int32), axis=1)
    at_rank = rank[None, :] == slot_ids[:, None]
    order = jnp.sum(jnp.where(at_rank, slot_ids[None, :], 0), axis=1)
    before = jnp.sum((rank[None, :] + 1 == slot_ids[:, None]) * (ids + 1)[None, :], axis=1)
    here = jnp.sum(jnp.where(at_rank, (ids + 1)[None, :], 0), axis=1)
    keep = (before == here).astype(jnp.float32)
    blocks = jnp.arange(TB_DEV, dtype=jnp.int32)
    last = jnp.maximum(jnp.sum((ids[None, :] <= blocks[:, None]).astype(jnp.int32), axis=1) - 1, 0)
    has = jnp.max((ids[None, :] == blocks[:, None]).astype(jnp.float32), axis=1)

    rows = -(-2 * mode_dev // 16) * 16
    factor = jnp.where((mode_index == 0) | (mode_index == NLON // 2), 1.0, 2.0).astype(jnp.float32)
    factor = lax.dynamic_slice_in_dim(factor, lax.axis_index("band") * mode_dev, mode_dev)
    scalars = (entry_of, source_of, order, keep, last, has, factor)
    tensors = (
        interp_weight,
        source_field,
        filter_weight,
        *lon_parts(mode_index, bands, rows),
        *lat_tables(nlat),
    )
    return layer(scalars, tensors, bands, slots, rows)


def solution(mesh):
    in_specs = (
        P(("grp", "band"), None, None),
        P("band", None, None),
        P("band", None),
        P("band"),
        P("band"),
        P("band"),
        P(),
        P(None, None, "band", None),
    )
    out_specs = P(("grp", "band"), None)
    return jax.shard_map(
        per_device, mesh=mesh, in_specs=in_specs, out_specs=out_specs, check_vma=False
    )
```
